512 devices in a mesh: dp: 64 (over x_lo, z, core), blk: 8 (over x_hi, y).
Axes of the slice: x: 4 (x_hi: 2, x_lo: 2; x = x_hi * 2 + x_lo), y: 4, z: 16, core: 2. Of those that a mesh axis runs over, the one named last changes fastest.
Arguments:
- pooled_grad: bfloat16 [32768, 64, 256], P(('dp', 'blk')), may hold values from -6 to 6
- bag_ids: int32 [64, 64, 8, 64, 4], P('dp', None, 'blk'), may hold values from 0 to 1023
- bag_lengths: int32 [64, 64, 8, 64], P('dp', None, 'blk'), may hold values from 1 to 4
- slot_table: int32 [64], replicated, may hold values from 0 to 63, each once
- layer_input: bfloat16 [32768, 128], P(('dp', 'blk')), may hold values from -100 to 100
- layer_grad_out: bfloat16 [32768, 4096], P(('dp', 'blk')), may hold values from -1 to 1
- left_stats: float32 [32, 1, 128, 128], P('blk', None, 'dp'), may hold values from -600 to 600
- right_stats: float32 [32, 1, 128, 128], P('blk', None, 'dp'), may hold values from -600 to 600
- left_root: float32 [32, 1, 128, 128], P('blk'), may hold values from -3 to 3
- right_root: float32 [32, 1, 128, 128], P('blk'), may hold values from -3 to 3
- second_moment: float32 [1, 128, 4096], P(None, None, 'blk'), may hold values from 0.01 to 10
Outputs:
- table_grad: float32 [64, 1024, 256], P('dp', 'blk')
- left_new: float32 [32, 1, 128, 128], P('blk', None, 'dp')
- right_new: float32 [32, 1, 128, 128], P('blk', None, 'dp')
- moment_new: float32 [1, 128, 4096], P(None, 'dp', 'blk')
- update: bfloat16 [1, 128, 4096], replicated
The draws below stay inside these ranges and needn't reach their ends.
All inputs are finite; a program needn't handle non-finite values.
Results may differ from the reference program's by a relative error of at most 0.001.
Values may be sent and summed in bfloat16 or wider, within the bound.
A program may use at most 128 MiB of HBM per device.

```python
import math
import jax
import jax.numpy as jnp
from jax import lax

EDIM = 256
POOL = 4
SAMP_DEV = 64
WIDTH = 4096
BS = 128
BLOCK_ROWS = 1
TABLES = 64
SAMPLES = 32768
ROWS = 1024
KIN = 128
NCOL = 32
N_DP = 64
N_BLK = 8


def root_matrix(key):
    first_key, second_key = jax.random.split(key)
    diagonal = jnp.exp(jax.random.uniform(first_key, (NCOL, BLOCK_ROWS, BS), jnp.float32, -0.69, 0.69))
    scatter_part = jax.random.uniform(second_key, (NCOL, BLOCK_ROWS, BS, BS), jnp.float32, -1.0, 1.0) / jnp.sqrt(jnp.float32(BS))
    symmetric = 0.5 * (scatter_part + jnp.swapaxes(scatter_part, 2, 3))
    identity = jnp.eye(BS, dtype=jnp.float32)
    return symmetric + identity * diagonal[..., None]


def draw_left_root(key, part):
    key = jax.random.fold_in(key, 21)
    return root_matrix(key)


def draw_right_root(key, part):
    key = jax.random.fold_in(key, 22)
    return root_matrix(key)


def draw_layer_input(key, part):
    key = jax.random.fold_in(key, 11)
    first_key, second_key = jax.random.split(key)
    shape = (SAMPLES, KIN)
    base = jnp.clip(jax.random.normal(first_key, shape, jnp.float32), -6.0, 6.0)
    top_scale = 10.0
    ramp = jnp.exp(jnp.log(top_scale) * jnp.arange(KIN, dtype=jnp.float32) / KIN)
    rough = jnp.exp(jax.random.uniform(second_key, (KIN,), jnp.float32, -0.4, 0.4))
    return (base * ramp * rough).astype(jnp.bfloat16)


def draw_layer_grad_out(key, part):
    key = jax.random.fold_in(key, 12)
    first_key, second_key = jax.random.split(key, 2)
    shape = (SAMPLES, WIDTH)
    column_scale = jnp.exp(jax.random.uniform(second_key, (WIDTH,), jnp.float32, -1.15, 1.15))
    base = jnp.clip(jax.random.normal(first_key, shape, jnp.float32), -6.0, 6.0)
    return (base * column_scale / jnp.sqrt(jnp.float32(SAMPLES))).astype(jnp.bfloat16)


def plant(array, rng, least, largest):
    shape = array.shape
    spot = [jax.random.randint(jax.random.fold_in(rng, axis), (), 0, shape[axis]) for axis in range(len(shape))]
    array = array.at[tuple(spot)].set(least)
    longest = shape.index(max(shape))
    spot[longest] = (spot[longest] + 1) % shape[longest]
    return array.at[tuple(spot)].set(largest)


def levels(rng, extent, cuts, low, largest):
    factor_of, own = 1.0, jax.random.fold_in(rng, 6)
    for axis_at, shards_of in cuts:
        heights = jnp.exp(jax.random.uniform(jax.random.fold_in(own, axis_at), (shards_of,), jnp.float32, low / len(cuts), largest / len(cuts)))
        factor_of = factor_of * jnp.repeat(heights, extent[axis_at] // shards_of).reshape([-1 if axis == axis_at else 1 for axis in range(len(extent))])
    return factor_of


def noise(rng, extent, deviation, reach, cuts=(), kind=jnp.bfloat16):
    values = jax.random.normal(rng, extent, jnp.float32) * deviation
    if len(cuts) > 0:
        values = levels(rng, extent, cuts, -0.22, 0.18) * values
    return jnp.clip(values, min=-reach, max=reach).astype(kind)


def setup_inputs(seed: int = 0) -> dict:
    seeds = jax.random.split(jax.random.key(seed), 12)
    pooled_grad = noise(seeds[0], (SAMPLES, TABLES, EDIM), 1.0, 6.0, ((0, 512),))
    bag_ids = plant(jax.random.randint(seeds[1], (TABLES, N_DP, N_BLK, SAMP_DEV, POOL), 0, ROWS), jax.random.fold_in(seeds[1], 1), 0, ROWS - 1).astype(jnp.int32)
    bag_lengths = plant(jax.random.randint(seeds[2], (TABLES, N_DP, N_BLK, SAMP_DEV), 1, POOL + 1), jax.random.fold_in(seeds[2], 1), 1, POOL).astype(jnp.int32)
    slot_table = jax.random.permutation(seeds[3], TABLES).astype(jnp.int32)
    layer_input = draw_layer_input(jax.random.fold_in(seeds[11], 71), 0)
    layer_grad_out = draw_layer_grad_out(jax.random.fold_in(seeds[11], 71), 0)
    left_stats = noise(seeds[6], (NCOL, BLOCK_ROWS, BS, BS), 100.0, 600.0, ((0, 8), (2, 64)), jnp.float32)
    right_stats = noise(seeds[7], (NCOL, BLOCK_ROWS, BS, BS), 100.0, 600.0, ((0, 8), (2, 64)), jnp.float32)
    left_root = draw_left_root(jax.random.fold_in(seeds[11], 71), 0)
    right_root = draw_right_root(jax.random.fold_in(seeds[11], 71), 0)
    second_moment = jnp.clip(jnp.exp(math.log(10.0) - 6.9077553 * jax.random.uniform(seeds[10], (BLOCK_ROWS, BS, WIDTH), jnp.float32) ** levels(seeds[10], (BLOCK_ROWS, BS, WIDTH), ((2, 8),), -0.2, 0.2)), 0.01, 10.0)
    return {"pooled_grad": pooled_grad, "bag_ids": bag_ids, "bag_lengths": bag_lengths, "slot_table": slot_table, "layer_input": layer_input, "layer_grad_out": layer_grad_out, "left_stats": left_stats, "right_stats": right_stats, "left_root": left_root, "right_root": right_root, "second_moment": second_moment}


second_beta = 0.9
graft_epsilon = 1e-08
norm_epsilon = 1e-06
highest = lax.Precision.HIGHEST

def to_blocks(matrix):
    shaped = matrix.reshape(BLOCK_ROWS, BS, NCOL, BS)
    return jnp.transpose(shaped, (2, 0, 1, 3))

def from_blocks(blocks):
    return jnp.transpose(blocks, (1, 2, 0, 3)).reshape(BLOCK_ROWS, BS, NCOL * BS)

def reference(pooled_grad, bag_ids, bag_lengths, slot_table, layer_input, layer_grad_out, left_stats, right_stats, left_root, right_root, second_moment):
    flat_ids = bag_ids.reshape(TABLES, SAMPLES, POOL)
    flat_lengths = bag_lengths.reshape(TABLES, SAMPLES)

    def one_table(operands):
        table_ids, table_lengths, table_index = operands
        column = jnp.take(pooled_grad, table_index, axis=1).astype(jnp.float32)
        inverse = 1.0 / table_lengths.astype(jnp.float32)
        accumulator = jnp.zeros((ROWS, EDIM), jnp.float32)
        for position in range(POOL):
            weight = jnp.where(position < table_lengths, inverse, jnp.zeros_like(inverse))
            accumulator = accumulator.at[table_ids[:, position]].add(column * weight[:, None])
        return accumulator
    table_grad = lax.map(one_table, (flat_ids, flat_lengths, slot_table))
    grad = jnp.dot(layer_input.T, layer_grad_out, preferred_element_type=jnp.float32)
    blocks = to_blocks(grad)
    left_new = left_stats + jnp.einsum('crij,crkj->crik', blocks, blocks, precision=highest)
    right_new = right_stats + jnp.einsum('crji,crjk->crik', blocks, blocks, precision=highest)
    halfway = jnp.einsum('crij,crjk->crik', left_root, blocks, precision=highest)
    precond = jnp.einsum('crij,crjk->crik', halfway, right_root, precision=highest)
    grad_rows = grad.reshape(BLOCK_ROWS, BS, WIDTH)
    moment_new = second_beta * second_moment + (1.0 - second_beta) * grad_rows * grad_rows
    graft_rows = grad_rows / (jnp.sqrt(moment_new) + graft_epsilon)
    graft = to_blocks(graft_rows.reshape(KIN, WIDTH))
    graft_square = lax.optimization_barrier(jnp.sum(graft * graft, axis=(2, 3)))
    precond_square = lax.optimization_barrier(jnp.sum(precond * precond, axis=(2, 3)))
    ratio = jnp.sqrt(graft_square / (precond_square + norm_epsilon))
    update = from_blocks(precond * ratio[:, :, None, None]).astype(jnp.bfloat16)
    return (table_grad, left_new, right_new, moment_new, update)
```

```python
import functools

import jax
import jax.numpy as jnp
from jax import lax
from jax.experimental import pallas as pl
from jax.experimental.pallas import tpu as pltpu
from jax.sharding import PartitionSpec as P

MESH = pl.DeviceIdType.MESH
F32, BF16 = jnp.float32, jnp.bfloat16
CORES, XLO = 2, 2
GROUP = CORES * XLO
POOL = 4
HALVES = 2

second_beta = 0.9
graft_epsilon = 1e-08
norm_epsilon = 1e-06
highest = lax.Precision.HIGHEST


def arrange_kernel(depth, columns, slots_ref, x_ref, ids_ref, len_ref, raw_ref, out_ids_ref, wide):
    samples, tables, edim = x_ref.shape
    width = edim // HALVES
    shares = depth // columns

    def widen(s, carry):
        rows = pl.ds(pl.multiple_of(s * tables, tables), tables)
        for h in range(HALVES):
            wide[h, rows, :] = x_ref[s, :, h * width : (h + 1) * width].astype(F32)
        return carry

    lax.fori_loop(0, samples, widen, 0)

    def pick(q, carry):
        col, g = q // GROUP, q % GROUP
        for i in range(shares):
            slot = ((g // CORES) * depth + col * shares + i) * CORES + g % CORES
            table = slots_ref[slot]
            for h in range(HALVES):
                rows = wide[h, pl.ds(table, samples, stride=tables), :]
                raw_ref[h, q, i] = rows.astype(BF16)
        return carry

    lax.fori_loop(0, columns * GROUP, pick, 0)
    position = lax.broadcasted_iota(jnp.int32, (POOL, samples), 0)

    def mask(z, carry):
        for xl in range(XLO):
            for core in range(CORES):
                source = (xl * depth + z) * CORES + core
                bag = len_ref[pl.ds(source, 1), :]
                kept = jnp.where(position < bag, ids_ref[source], -1)
                out_ids_ref[z, xl * POOL : (xl + 1) * POOL, core * samples : (core + 1) * samples] = kept
        return carry

    lax.fori_loop(0, depth, mask, 0)


def main_kernel(
    depth,
    columns,
    raw_ref,
    ids_ref,
    x_ref,
    y_ref,
    left_stats_ref,
    right_stats_ref,
    left_root_ref,
    right_root_ref,
    moment_ref,
    table_ref,
    left_ref,
    right_ref,
    moment_new_ref,
    update_ref,
    idr,
    onehot,
    raw,
    up,
    down,
    final,
    xr,
    yr,
    part,
    parts,
    own_sum,
    grad,
    lmat,
    rmat,
    mmat,
    stage,
    stats,
    block_update,
    ids_sem,
    raw_sem,
    dense_sem,
    up_sem,
    down_sem,
    table_sem,
    parts_sem,
    grad_sem,
    stats_sem,
    update_sem,
    send_sem,
):
    plane = columns * GROUP
    shares = depth // columns
    half = depth // 2
    bs = lmat.shape[0]
    share = left_ref.shape[2]
    dp, blk = lax.axis_index("dp"), lax.axis_index("blk")
    core = dp % CORES
    z = (dp // CORES) % depth
    xl = dp // (CORES * depth)
    g = xl * CORES + core
    me = blk * GROUP + g

    def dp_of(xl_of, z_of, core_of):
        return (xl_of * depth + z_of) * CORES + core_of

    def in_plane(q):
        other = q % GROUP
        return (dp_of(other // CORES, z, other % CORES), q // GROUP)

    def along_z(z_of):
        return (dp_of(xl, z_of, core), blk)

    def loop(first, last, body):
        def step(k, carry):
            body(k)
            return carry

        lax.fori_loop(first, last, step, 0)

    def remote(src, dst, sent, arrived, device):
        return pltpu.make_async_remote_copy(
            src_ref=src, dst_ref=dst, send_sem=sent, recv_sem=arrived, device_id=device, device_id_type=MESH
        )

    def drain(ref, sem):
        pltpu.make_async_copy(ref, ref, sem).wait()

    ids_self = blk == z // shares
    piece_z = blk * shares + z // columns
    piece_blk = z % columns
    piece_self = jnp.logical_and(piece_z == z, piece_blk == blk)
    from_z = (z % shares) * columns + blk
    from_blk = z // shares

    barrier = pltpu.get_barrier_semaphore()

    def greet(device):
        pl.semaphore_signal(barrier, inc=1, device_id=device, device_id_type=MESH)

    loop(1, plane, lambda o: greet(in_plane((me + o) % plane)))
    loop(1, depth, lambda o: greet(along_z((z + o) % depth)))

    def greet_ids(k):
        z_of, blk_of = blk * shares + k // columns, k % columns

        @pl.when(jnp.logical_not(jnp.logical_and(z_of == z, blk_of == blk)))
        def _():
            greet((dp_of(xl, z_of, core), blk_of))

    loop(0, depth, greet_ids)

    @pl.when(jnp.logical_not(piece_self))
    def _():
        greet((dp_of(xl, from_z, core), from_blk))

    greetings = (plane - 1) + (depth - 1) + depth + 1
    pl.semaphore_wait(barrier, greetings - ids_self.astype(jnp.int32) - piece_self.astype(jnp.int32))

    def send_ids(k):
        z_of = (z + k) % depth
        itself = jnp.logical_and(z_of == z, ids_self)
        place = idr.at[z % shares, blk]

        @pl.when(itself)
        def _():
            pltpu.make_async_copy(ids_ref.at[z_of], place, ids_sem).start()

        @pl.when(jnp.logical_not(itself))
        def _():
            remote(ids_ref.at[z_of], place, send_sem.at[0], ids_sem, (dp_of(xl, z_of, core), z // shares)).start()

    loop(0, depth, send_ids)

    def send_raw(h):
        pltpu.make_async_copy(raw_ref.at[h, me], raw.at[h, me], raw_sem.at[h]).start()

        def one(o):
            q = (me + o) % plane
            remote(raw_ref.at[h, q], raw.at[h, me], send_sem.at[1], raw_sem.at[h], in_plane(q)).start()

        loop(1, plane, one)

    def send_dense():
        def y_part(q):
            return y_ref.at[:, pl.ds(pl.multiple_of(q * bs, bs), bs)]

        pltpu.make_async_copy(x_ref, xr.at[me], dense_sem.at[0]).start()
        pltpu.make_async_copy(y_part(me), yr.at[me], dense_sem.at[1]).start()

        def one(o):
            q = (me + o) % plane
            remote(x_ref, xr.at[me], send_sem.at[2], dense_sem.at[0], in_plane(q)).start()
            remote(y_part(q), yr.at[me], send_sem.at[3], dense_sem.at[1], in_plane(q)).start()

        loop(1, plane, one)

    send_raw(0)
    send_dense()
    send_raw(1)

    drain(idr, ids_sem)
    rows = lax.broadcasted_iota(jnp.int32, (bs, 128), 0)

    def weigh(k):
        i, source = k // columns, k % columns
        tile = idr[i, source]
        for x_of in range(XLO):
            ids = [tile[x_of * POOL + p : x_of * POOL + p + 1, :] for p in range(POOL)]
            length = sum((one >= 0).astype(jnp.int32) for one in ids)
            value = jnp.where(length == 1, 12.0, jnp.where(length == 2, 6.0, jnp.where(length == 3, 4.0, 3.0)))
            value = jnp.broadcast_to(value, (bs, 128))
            place = pl.ds(pl.multiple_of((source * XLO + x_of) * 128, 128), 128)
            ids = [jnp.broadcast_to(one, (bs, 128)) - rows for one in ids]
            for rb in range(columns):
                weight = jnp.zeros((bs, 128), F32)
                for one in ids:
                    weight = weight + jnp.where(one == rb * bs, value, 0.0)
                onehot[i, rb, :, place] = weight.astype(BF16)

    loop(0, shares * columns, weigh)

    def product(h, p):
        i, rb = p // columns, p % columns
        columns_of = raw[h, :, i].reshape(onehot.shape[3], 128)
        return jnp.dot(onehot[i, rb], columns_of, preferred_element_type=F32)

    def send_up(h, t):
        remote(
            up.at[h, t], up.at[h, t + 1], send_sem.at[4], up_sem.at[h, t + 1], along_z((z + 1) % depth)
        ).start()

    def send_down(h, t):
        remote(
            down.at[h, t], down.at[h, t + 1], send_sem.at[5], down_sem.at[h, t + 1], along_z((z + depth - 1) % depth)
        ).start()

    def piece_up(t):
        return (z + half - t + depth) % depth

    def piece_down(t):
        return (z - (half - 1) + t + depth) % depth

    def wait_up(h, t):
        drain(up.at[h, t], up_sem.at[h, t])

    def wait_down(h, t):
        drain(down.at[h, t], down_sem.at[h, t])

    for h in range(HALVES):
        drain(raw.at[h], raw_sem.at[h])
        up[h, 0] = product(h, piece_up(0))
        send_up(h, 0)
        down[h, 0] = product(h, piece_down(0))
        send_down(h, 0)

    def hop(t):
        for h in range(HALVES):
            first, second = product(h, piece_up(t)), product(h, piece_down(t))
            wait_up(h, t)
            up[h, t] += first
            send_up(h, t)
            wait_down(h, t)
            down[h, t] += second
            send_down(h, t)

    def dense_one():
        drain(xr, dense_sem.at[0])
        drain(yr, dense_sem.at[1])
        x_all = xr[...].reshape(onehot.shape[3], bs)
        y_all = yr[...].reshape(onehot.shape[3], bs)
        partial = lax.dot_general(x_all, y_all, (((0,), (0,)), ((), ())), preferred_element_type=F32)
        part[...] = partial.reshape(part.shape)

        def one(o):
            z_of = (z + o) % depth
            remote(part.at[z_of], parts.at[z], send_sem.at[6], parts_sem, along_z(z_of)).start()

        loop(1, depth, one)

    def dense_two():
        drain(parts.at[0 : depth - 1], parts_sem)
        parts[z] = part[z]
        own_sum[...] = jnp.sum(parts[...], axis=0)

        def one(o):
            remote(own_sum, grad.at[z], send_sem.at[7], grad_sem, along_z((z + o) % depth)).start()

        loop(1, depth, one)

    def dense_three():
        drain(grad.at[0 : depth - 1], grad_sem)
        grad[z] = own_sum[...]
        block = grad[...].reshape(bs, bs)
        moment_here = moment_ref[0, :, pl.ds(pl.multiple_of(g * bs, bs), bs)]
        moment = second_beta * moment_here + (1.0 - second_beta) * block * block
        graft = block / (jnp.sqrt(moment) + graft_epsilon)
        halfway = jnp.dot(left_root_ref[g, 0], block, precision=highest, preferred_element_type=F32)
        precond = jnp.dot(halfway, right_root_ref[g, 0], precision=highest, preferred_element_type=F32)
        ratio = jnp.sqrt(jnp.sum(graft * graft) / (jnp.sum(precond * precond) + norm_epsilon))
        block_update[...] = (precond * ratio).astype(BF16)
        place = update_ref.at[:, pl.ds(pl.multiple_of(me * bs, bs), bs)]
        pltpu.make_async_copy(block_update, place, update_sem).start()

        def one(o):
            remote(block_update, place, send_sem.at[8], update_sem, in_plane((me + o) % plane)).start()

        loop(1, plane, one)
        mmat[...] = moment
        lmat[...] = lax.dot_general(
            block, block, (((1,), (1,)), ((), ())), precision=highest, preferred_element_type=F32
        )
        rmat[...] = lax.dot_general(
            block, block, (((0,), (0,)), ((), ())), precision=highest, preferred_element_type=F32
        )
        stage[...] = jnp.zeros(stage.shape, F32)

        def rows_for(o):
            other = (g + o) % GROUP
            first = dp_of(other // CORES, z, other % CORES) * share
            for kind, matrix in enumerate((lmat, rmat, mmat)):
                for r in range(share):
                    stage[other, kind, r : r + 1, :] = matrix[pl.ds(first + r, 1), :]

        loop(0, GROUP, rows_for)

        def one_group(o):
            other = (g + o) % GROUP
            remote(stage.at[other], stats.at[g], send_sem.at[9], stats_sem, in_plane(blk * GROUP + other)).start()

        loop(1, GROUP, one_group)

    def dense_four():
        drain(stats.at[0 : GROUP - 1], stats_sem)
        stats[g] = stage[g]
        for other in range(GROUP):
            left_ref[other, 0] = left_stats_ref[other, 0] + stats[other, 0, 0:share, :]
            right_ref[other, 0] = right_stats_ref[other, 0] + stats[other, 1, 0:share, :]
            moment_new_ref[0, :, other * bs : (other + 1) * bs] = stats[other, 2, 0:share, :]

    steps = half - 1
    cut_one = min(2, steps)
    cut_two = min(5, steps)
    dense_one()
    loop(1, cut_one, hop)
    dense_two()
    loop(cut_one, cut_two, hop)
    dense_three()
    loop(cut_two, steps, hop)

    for h in range(HALVES):
        first, second = product(h, piece_up(half - 1)), product(h, z)
        wait_up(h, half - 1)
        up[h, half - 1] += first
        send_up(h, half - 1)
        wait_down(h, half - 1)
        final[h] = down[h, half - 1] + second
    for h in range(HALVES):
        wait_up(h, half)
        final[h] = (final[h] + up[h, half]) * (1.0 / 12.0)
        place = table_ref.at[:, h * 128 : (h + 1) * 128]

        @pl.when(piece_self)
        def _():
            pltpu.make_async_copy(final.at[h], place, table_sem).start()

        @pl.when(jnp.logical_not(piece_self))
        def _():
            remote(final.at[h], place, send_sem.at[10], table_sem, (dp_of(xl, piece_z, core), piece_blk)).start()

    dense_four()
    drain(update_ref, update_sem)
    drain(table_ref, table_sem)

    @pl.when(ids_self)
    def _():
        drain(ids_ref.at[0 : depth - 1], send_sem.at[0])

    @pl.when(jnp.logical_not(ids_self))
    def _():
        drain(ids_ref, send_sem.at[0])

    for h in range(HALVES):
        drain(raw.at[h, 0 : plane - 1], send_sem.at[1])
    drain(xr.at[0 : plane - 1], send_sem.at[2])
    drain(yr.at[0 : plane - 1], send_sem.at[3])
    drain(up.at[:, 0:half], send_sem.at[4])
    if half > 1:
        drain(down.at[:, 0 : half - 1], send_sem.at[5])
    drain(parts.at[0 : depth - 1], send_sem.at[6])
    drain(grad.at[0 : depth - 1], send_sem.at[7])
    drain(update_ref.at[:, 0 : (plane - 1) * bs], send_sem.at[8])
    drain(stats.at[0 : GROUP - 1], send_sem.at[9])

    @pl.when(jnp.logical_not(piece_self))
    def _():
        drain(final, send_sem.at[10])


def per_device(
    pooled_grad,
    bag_ids,
    bag_lengths,
    slot_table,
    layer_input,
    layer_grad_out,
    left_stats,
    right_stats,
    left_root,
    right_root,
    second_moment,
):
    depth = lax.axis_size("dp") // GROUP
    columns = lax.axis_size("blk")
    plane = columns * GROUP
    shares = depth // columns
    half = depth // 2
    samples, tables, edim = pooled_grad.shape
    width = edim // HALVES
    bs = left_root.shape[2]
    share = left_stats.shape[2]
    kdim = layer_input.shape[1]
    ids = jnp.transpose(bag_ids, (0, 1, 2, 4, 3)).reshape(tables, POOL, samples)
    lengths = bag_lengths.reshape(tables, samples)
    vmem = pl.BlockSpec(memory_space=pltpu.VMEM)
    smem = pl.BlockSpec(memory_space=pltpu.SMEM)
    hbm = pl.BlockSpec(memory_space=pl.ANY)
    raw, masked = pl.pallas_call(
        functools.partial(arrange_kernel, depth, columns),
        out_shape=(
            jax.ShapeDtypeStruct((HALVES, plane, shares, samples, width), BF16),
            jax.ShapeDtypeStruct((depth, XLO * POOL, CORES * samples), jnp.int32),
        ),
        in_specs=[smem, vmem, vmem, vmem],
        out_specs=(vmem, vmem),
        scratch_shapes=[pltpu.VMEM((HALVES, samples * tables, width), F32)],
        compiler_params=pltpu.CompilerParams(vmem_limit_bytes=32 * 1024 * 1024),
        name="arrange",
    )(slot_table, pooled_grad, ids, lengths)
    dma = pltpu.SemaphoreType.DMA
    table, left_new, right_new, moment_new, update = pl.pallas_call(
        functools.partial(main_kernel, depth, columns),
        out_shape=(
            jax.ShapeDtypeStruct((bs, edim), F32),
            jax.ShapeDtypeStruct(left_stats.shape, F32),
            jax.ShapeDtypeStruct(right_stats.shape, F32),
            jax.ShapeDtypeStruct((1, share, GROUP * bs), F32),
            jax.ShapeDtypeStruct((bs, plane * bs), BF16),
        ),
        in_specs=[hbm, hbm, hbm, hbm, vmem, vmem, vmem, vmem, vmem],
        out_specs=(hbm, vmem, vmem, vmem, hbm),
        scratch_shapes=[
            pltpu.VMEM((shares, columns, XLO * POOL, CORES * samples), jnp.int32),
            pltpu.VMEM((shares, columns, bs, plane * samples), BF16),
            pltpu.VMEM((HALVES, plane, shares, samples, width), BF16),
            pltpu.VMEM((HALVES, half + 1, bs, width), F32),
            pltpu.VMEM((HALVES, half, bs, width), F32),
            pltpu.VMEM((HALVES, bs, width), F32),
            pltpu.VMEM((plane, samples, kdim), BF16),
            pltpu.VMEM((plane, samples, bs), BF16),
            pltpu.VMEM((depth, bs // depth, bs), F32),
            pltpu.VMEM((depth, bs // depth, bs), F32),
            pltpu.VMEM((bs // depth, bs), F32),
            pltpu.VMEM((depth, bs // depth, bs), F32),
            pltpu.VMEM((bs, bs), F32),
            pltpu.VMEM((bs, bs), F32),
            pltpu.VMEM((bs, bs), F32),
            pltpu.VMEM((GROUP, 3, 8, bs), F32),
            pltpu.VMEM((GROUP, 3, 8, bs), F32),
            pltpu.VMEM((bs, bs), BF16),
            dma,
            dma((HALVES,)),
            dma((2,)),
            dma((HALVES, half + 1)),
            dma((HALVES, half)),
            dma,
            dma,
            dma,
            dma,
            dma,
            dma((11,)),
        ],
        compiler_params=pltpu.CompilerParams(
            collective_id=0, has_side_effects=True, vmem_limit_bytes=48 * 1024 * 1024
        ),
        name="exchange",
    )(
        raw,
        masked,
        layer_input,
        layer_grad_out,
        left_stats,
        right_stats,
        left_root,
        right_root,
        second_moment,
    )
    return table[None], left_new, right_new, moment_new, update[None]


def solution(mesh):
    placed = (
        P(("dp", "blk"), None, None),
        P("dp", None, "blk", None, None),
        P("dp", None, "blk", None),
        P(),
        P(("dp", "blk"), None),
        P(("dp", "blk"), None),
        P("blk", None, "dp", None),
        P("blk", None, "dp", None),
        P("blk", None, None, None),
        P("blk", None, None, None),
        P(None, None, "blk"),
    )
    return jax.shard_map(
        per_device,
        mesh=mesh,
        in_specs=placed,
        out_specs=(
            P("dp", "blk", None),
            P("blk", None, "dp", None),
            P("blk", None, "dp", None),
            P(None, "dp", "blk"),
            P(),
        ),
        check_vma=False,
    )
```

```python
import functools

import jax
import jax.numpy as jnp
from jax import lax
from jax.experimental import pallas as pl
from jax.experimental.pallas import tpu as pltpu
from jax.sharding import PartitionSpec as P

MESH = pl.DeviceIdType.MESH
F32, BF16 = jnp.float32, jnp.bfloat16
CORES, XLO = 2, 2
GROUP = CORES * XLO
POOL = 4
HALVES = 2
LAG = 5
DENSE_AT = (2, 3, 5, 7, 8, 10, 13)
SUBS = 4

second_beta = 0.9
graft_epsilon = 1e-08
norm_epsilon = 1e-06
highest = lax.Precision.HIGHEST


def exchange_kernel(
    depth,
    columns,
    slots_ref,
    pooled_ref,
    ids_ref,
    lengths_ref,
    x_ref,
    y_ref,
    left_stats_ref,
    right_stats_ref,
    left_root_ref,
    right_root_ref,
    moment_ref,
    table_ref,
    left_ref,
    right_ref,
    moment_new_ref,
    update_ref,
    pooled,
    wide,
    ordered,
    ids_in,
    lengths_in,
    masked,
    idr,
    onehot,
    raw,
    own,
    up,
    down,
    final,
    xr,
    yr,
    part,
    parts,
    own_sum,
    grad,
    lmat,
    rmat,
    mmat,
    stage,
    stats,
    block_update,
    left_root,
    right_root,
    moment_in,
    left_stats,
    right_stats,
    left_out,
    right_out,
    moment_out,
    pooled_sem,
    in_sem,
    out_sem,
    ids_sem,
    raw_sem,
    x_sem,
    y_sem,
    up_sem,
    down_sem,
    table_sem,
    parts_sem,
    grad_sem,
    stats_sem,
    update_sem,
    passed_sem,
    send_sem,
):
    plane = columns * GROUP
    chips = plane // CORES
    shares = depth // columns
    half = depth // 2
    bs = lmat.shape[0]
    share = left_ref.shape[2]
    samples, tables, edim = pooled.shape
    width = edim // HALVES
    kdim = plane * samples
    dp, blk = lax.axis_index("dp"), lax.axis_index("blk")
    core = dp % CORES
    z = (dp // CORES) % depth
    xl = dp // (CORES * depth)
    g = xl * CORES + core
    me = blk * GROUP + g
    chip = me // CORES

    def dp_of(xl_of, z_of, core_of):
        return (xl_of * depth + z_of) * CORES + core_of

    def in_plane(q):
        other = q % GROUP
        return (dp_of(other // CORES, z, other % CORES), q // GROUP)

    def along_z(z_of):
        return (dp_of(xl, z_of, core), blk)

    def same_core(chip_of):
        return in_plane(chip_of * CORES + core)

    twin = in_plane(chip * CORES + 1 - core)

    def loop(first, last, body):
        def step(k, carry):
            body(k)
            return carry

        lax.fori_loop(first, last, step, 0)

    def remote(src, dst, sent, arrived, device):
        return pltpu.make_async_remote_copy(
            src_ref=src, dst_ref=dst, send_sem=sent, recv_sem=arrived, device_id=device, device_id_type=MESH
        )

    def drain(ref, sem):
        pltpu.make_async_copy(ref, ref, sem).wait()

    chunks = pooled_sem.shape[0]
    per_chunk = samples // chunks

    def pooled_copy(k):
        rows = pl.ds(k * per_chunk, per_chunk)
        return pltpu.make_async_copy(pooled_ref.at[rows], pooled.at[rows], pooled_sem.at[k])

    local = [
        pltpu.make_async_copy(src, dst, in_sem.at[k])
        for k, (src, dst) in enumerate(
            (
                (ids_ref, ids_in),
                (lengths_ref, lengths_in),
                (left_root_ref.at[g, 0], left_root),
                (right_root_ref.at[g, 0], right_root),
                (moment_ref.at[0, :, pl.ds(pl.multiple_of(g * bs, bs), bs)], moment_in),
                (left_stats_ref, left_stats),
                (right_stats_ref, right_stats),
            )
        )
    ]
    loop(0, chunks, lambda k: pooled_copy(k).start())
    for copy in local:
        copy.start()

    ids_self = blk == z // shares
    piece_z = blk * shares + z // columns
    piece_blk = z % columns
    piece_self = jnp.logical_and(piece_z == z, piece_blk == blk)
    from_z = (z % shares) * columns + blk
    from_blk = z // shares

    barrier = pltpu.get_barrier_semaphore()

    def greet(device):
        pl.semaphore_signal(barrier, inc=1, device_id=device, device_id_type=MESH)

    loop(1, plane, lambda o: greet(in_plane((me + o) % plane)))
    loop(1, depth, lambda o: greet(along_z((z + o) % depth)))

    def greet_ids(k):
        z_of, blk_of = blk * shares + k // columns, k % columns

        @pl.when(jnp.logical_not(jnp.logical_and(z_of == z, blk_of == blk)))
        def _():
            greet((dp_of(xl, z_of, core), blk_of))

    loop(0, depth, greet_ids)

    @pl.when(jnp.logical_not(piece_self))
    def _():
        greet((dp_of(xl, from_z, core), from_blk))

    local[0].wait()
    local[1].wait()
    position = lax.broadcasted_iota(jnp.int32, (POOL, samples), 0)

    def mask(z_of):
        for x_of in range(XLO):
            for core_of in range(CORES):
                source = dp_of(x_of, z_of, core_of)
                bag = lengths_in[pl.ds(source, 1), :]
                kept = jnp.where(position < bag, ids_in[source], -1)
                masked[z_of, x_of * POOL : (x_of + 1) * POOL, core_of * samples : (core_of + 1) * samples] = kept

    loop(0, depth, mask)

    def widen(h):
        def one(s):
            rows = pl.ds(pl.multiple_of(s * tables, tables), tables)
            wide[h, rows, :] = pooled[s, :, h * width : (h + 1) * width].astype(F32)

        return one

    def widen_first(k):
        pooled_copy(k).wait()
        loop(k * per_chunk, (k + 1) * per_chunk, widen(0))

    loop(0, chunks, widen_first)

    greetings = (plane - 1) + (depth - 1) + depth + 1
    pl.semaphore_wait(barrier, greetings - ids_self.astype(jnp.int32) - piece_self.astype(jnp.int32))

    def send_ids(k):
        z_of = (z + k) % depth
        itself = jnp.logical_and(z_of == z, ids_self)
        place = idr.at[z % shares, blk]

        @pl.when(itself)
        def _():
            pltpu.make_async_copy(masked.at[z_of], place, ids_sem).start()

        @pl.when(jnp.logical_not(itself))
        def _():
            remote(masked.at[z_of], place, send_sem.at[0], ids_sem, (dp_of(xl, z_of, core), z // shares)).start()

    loop(0, depth, send_ids)

    def rows_of(h, q, i):
        other = q % GROUP
        slot = dp_of(other // CORES, (q // GROUP) * shares + i, other % CORES)
        return wide[h, pl.ds(slots_ref[slot], samples, stride=tables), :].astype(BF16)

    def send_raw(h):
        def one(o):
            q = (me + o) % plane
            for i in range(shares):
                ordered[h, q, i] = rows_of(h, q, i)
            remote(ordered.at[h, q], raw.at[h, me], send_sem.at[1], raw_sem.at[h], in_plane(q)).start()

        loop(1, plane, one)
        for i in range(shares):
            raw[h, me, i] = rows_of(h, me, i)

    def send_dense():
        def y_part(q):
            return y_ref.at[:, pl.ds(pl.multiple_of(q * bs, bs), bs)]

        pltpu.make_async_copy(x_ref, xr.at[core, chip], x_sem.at[0]).start()
        pltpu.make_async_copy(y_part(me), yr.at[core, chip], y_sem).start()

        def one_x(o):
            remote(x_ref, xr.at[core, chip], send_sem.at[2], x_sem.at[0], same_core((chip + o) % chips)).start()

        def one_y(o):
            q = (me + o) % plane
            remote(y_part(q), yr.at[core, chip], send_sem.at[3], y_sem, in_plane(q)).start()

        loop(1, chips, one_x)
        loop(1, plane, one_y)

    send_raw(0)
    send_dense()
    loop(0, samples, widen(1))
    send_raw(1)

    drain(idr, ids_sem)
    rows = lax.broadcasted_iota(jnp.int32, (bs, 128), 0)

    def weigh(k):
        i, source = k // columns, k % columns
        tile = idr[i, source]
        for x_of in range(XLO):
            ids = [tile[x_of * POOL + p : x_of * POOL + p + 1, :] for p in range(POOL)]
            length = sum((one >= 0).astype(jnp.int32) for one in ids)
            value = jnp.where(length == 1, 12.0, jnp.where(length == 2, 6.0, jnp.where(length == 3, 4.0, 3.0)))
            value = jnp.broadcast_to(value, (bs, 128))
            place = pl.ds(pl.multiple_of((source * XLO + x_of) * 128, 128), 128)
            ids = [jnp.broadcast_to(one, (bs, 128)) - rows for one in ids]
            for rb in range(columns):
                weight = jnp.zeros((bs, 128), F32)
                for one in ids:
                    weight = weight + jnp.where(one == rb * bs, value, 0.0)
                onehot[i, rb * bs : (rb + 1) * bs, place] = weight.astype(BF16)

    loop(0, shares * columns, weigh)

    def product(h, i):
        whole = jnp.dot(onehot[i], raw[h, :, i].reshape(kdim, width), preferred_element_type=F32)
        own[h, pl.ds(i * columns, columns)] = whole.reshape(columns, bs, width)

    def product_of(h, p):
        i, rb = p // columns, p % columns
        weights = onehot[i, pl.ds(pl.multiple_of(rb * bs, bs), bs), :]
        own[h, p] = jnp.dot(weights, raw[h, :, i].reshape(kdim, width), preferred_element_type=F32)

    sub = bs // SUBS

    def rows_at(s):
        return pl.ds(s * sub, sub)

    def send_up(h, t, s):
        there = up.at[h, t + 1, rows_at(s)]
        remote(
            up.at[h, t, rows_at(s)], there, send_sem.at[4], up_sem.at[h, t + 1, s], along_z((z + 1) % depth)
        ).start()

    def send_down(h, t, s):
        there = down.at[h, t + 1, rows_at(s)]
        remote(
            down.at[h, t, rows_at(s)], there, send_sem.at[5], down_sem.at[h, t + 1, s], along_z((z + depth - 1) % depth)
        ).start()

    def piece_up(t):
        return (z + half - t + depth) % depth

    def piece_down(t):
        return (z - (half - 1) + t + depth) % depth

    def wait_up(h, t, s):
        drain(up.at[h, t, rows_at(s)], up_sem.at[h, t, s])

    def wait_down(h, t, s):
        drain(down.at[h, t, rows_at(s)], down_sem.at[h, t, s])

    def begin(h):
        drain(raw.at[h, 0 : plane - 1], raw_sem.at[h])
        for k in range(shares):
            if h == 0:
                product(h, (piece_up(0) // columns + k) % shares)
            elif k == 0:
                product_of(h, piece_up(0))
            if k == 0:
                up[h, 0] = own[h, piece_up(0)]
                for s in range(SUBS):
                    send_up(h, 0, s)
        if h > 0:
            product_of(h, piece_down(0))
        down[h, 0] = own[h, piece_down(0)]
        if half > 1:
            for s in range(SUBS):
                send_down(h, 0, s)

    def hop(h, t):
        if h > 0:
            product_of(h, piece_up(t))
            product_of(h, piece_down(t))
        for s in range(SUBS):
            wait_up(h, t, s)
            up[h, t, rows_at(s)] += own[h, piece_up(t), rows_at(s)]
            send_up(h, t, s)
            wait_down(h, t, s)
            down[h, t, rows_at(s)] += own[h, piece_down(t), rows_at(s)]
            send_down(h, t, s)

    def last(h):
        t = half - 1
        if h > 0:
            product_of(h, piece_up(t))
            product_of(h, z)
        for s in range(SUBS):
            wait_up(h, t, s)
            up[h, t, rows_at(s)] += own[h, piece_up(t), rows_at(s)]
            send_up(h, t, s)
        for s in range(SUBS):
            wait_down(h, t, s)
            final[h, rows_at(s)] = down[h, t, rows_at(s)] + own[h, z, rows_at(s)]

    def finish(h):
        for s in range(SUBS):
            wait_up(h, half, s)
            final[h, rows_at(s)] = (final[h, rows_at(s)] + up[h, half, rows_at(s)]) * (1.0 / 12.0)
            piece = final.at[h, rows_at(s)]
            place = table_ref.at[rows_at(s), h * width : (h + 1) * width]

            @pl.when(piece_self)
            def _(piece=piece, place=place):
                pltpu.make_async_copy(piece, place, table_sem).start()

            @pl.when(jnp.logical_not(piece_self))
            def _(piece=piece, place=place):
                remote(piece, place, send_sem.at[10], table_sem, (dp_of(xl, piece_z, core), piece_blk)).start()

    def pass_input():
        drain(xr.at[core], x_sem.at[0])
        remote(xr.at[core], xr.at[core], send_sem.at[11], x_sem.at[1], twin).start()

    def dense_one():
        drain(yr, y_sem)
        drain(xr.at[core], x_sem.at[1])
        partial = lax.dot_general(
            xr[...].reshape(kdim, bs),
            yr[...].reshape(kdim, bs),
            (((0,), (0,)), ((), ())),
            preferred_element_type=F32,
        )
        part[...] = partial.reshape(part.shape)

        def one(o):
            z_of = (z + o) % depth
            remote(part.at[z_of], parts.at[z], send_sem.at[6], parts_sem, along_z(z_of)).start()

        loop(1, depth, one)

    def dense_two():
        drain(parts.at[0 : depth - 1], parts_sem)
        parts[z] = part[z]
        own_sum[...] = jnp.sum(parts[...], axis=0)

        def one(o):
            remote(own_sum, grad.at[z], send_sem.at[7], grad_sem, along_z((z + o) % depth)).start()

        loop(1, depth, one)

    def block_place(q):
        return update_ref.at[:, pl.ds(pl.multiple_of(q * bs, bs), bs)]

    def dense_three():
        drain(grad.at[0 : depth - 1], grad_sem)
        grad[z] = own_sum[...]
        block = grad[...].reshape(bs, bs)
        for copy in local[2:5]:
            copy.wait()
        moment = second_beta * moment_in[...] + (1.0 - second_beta) * block * block
        graft = block / (jnp.sqrt(moment) + graft_epsilon)
        halfway = jnp.dot(left_root[...], block, precision=highest, preferred_element_type=F32)
        precond = jnp.dot(halfway, right_root[...], precision=highest, preferred_element_type=F32)
        ratio = jnp.sqrt(jnp.sum(graft * graft) / (jnp.sum(precond * precond) + norm_epsilon))
        block_update[...] = (precond * ratio).astype(BF16)
        place = block_place(me)

        def one(o):
            remote(block_update, place, send_sem.at[8], update_sem.at[o], same_core((chip + o) % chips)).start()

        loop(1, chips, one)
        remote(block_update, place, send_sem.at[8], passed_sem, twin).start()
        pltpu.make_async_copy(block_update, place, update_sem.at[0]).start()
        mmat[...] = moment

    def statistics():
        block = grad[...].reshape(bs, bs)
        lmat[...] = lax.dot_general(
            block, block, (((1,), (1,)), ((), ())), precision=highest, preferred_element_type=F32
        )
        rmat[...] = lax.dot_general(
            block, block, (((0,), (0,)), ((), ())), precision=highest, preferred_element_type=F32
        )
        stage[...] = jnp.zeros(stage.shape, F32)

        def rows_for(o):
            other = (g + o) % GROUP
            first = dp_of(other // CORES, z, other % CORES) * share
            for kind, matrix in enumerate((lmat, rmat, mmat)):
                for r in range(share):
                    stage[other, kind, r : r + 1, :] = matrix[pl.ds(first + r, 1), :]

        loop(0, GROUP, rows_for)

        def one_group(o):
            other = (g + o) % GROUP
            remote(stage.at[other], stats.at[g], send_sem.at[9], stats_sem, in_plane(blk * GROUP + other)).start()

        loop(1, GROUP, one_group)

    def pass_update():
        def one(o):
            place = block_place(((chip + chips - o) % chips) * CORES + core)
            pltpu.make_async_copy(place, place, update_sem.at[o]).wait()
            remote(place, place, send_sem.at[8], passed_sem, twin).start()

        loop(1, chips, one)

    results = (
        pltpu.make_async_copy(left_out, left_ref, out_sem.at[0]),
        pltpu.make_async_copy(right_out, right_ref, out_sem.at[1]),
        pltpu.make_async_copy(moment_out, moment_new_ref, out_sem.at[2]),
    )

    def store_statistics():
        local[5].wait()
        local[6].wait()
        drain(stats.at[0 : GROUP - 1], stats_sem)
        stats[g] = stage[g]
        for other in range(GROUP):
            left_out[other, 0] = left_stats[other, 0] + stats[other, 0, 0:share, :]
            right_out[other, 0] = right_stats[other, 0] + stats[other, 1, 0:share, :]
            moment_out[0, :, other * bs : (other + 1) * bs] = stats[other, 2, 0:share, :]
        for copy in results:
            copy.start()

    lag = min(LAG, half + 1)
    end = half + lag
    dense = {}
    parts_of_dense = (pass_input, dense_one, dense_two, dense_three, statistics, pass_update, store_statistics)
    for at, part_of in zip(DENSE_AT, parts_of_dense):
        dense.setdefault(min(at, end), []).append(part_of)

    def kind(t):
        return "" if t < 0 or t > half else "b" if t == 0 else "f" if t == half else "l" if t == half - 1 else "h"

    step = 0
    while step <= end:
        kinds = (kind(step), kind(step - lag))
        stop = step + 1
        while stop <= end and "h" in kinds and (kind(stop), kind(stop - lag)) == kinds and not dense.get(stop - 1):
            stop += 1

        def run(t, kinds=kinds):
            for h, what in enumerate(kinds):
                if what == "b":
                    begin(h)
                elif what == "h":
                    hop(h, t - h * lag)
                elif what == "l":
                    last(h)
                elif what == "f":
                    finish(h)

        if stop - step > 1:
            loop(step, stop, run)
        else:
            run(step)
        for part_of in dense.get(stop - 1, ()):
            part_of()
        step = stop

    drain(table_ref, table_sem)
    drain(block_place(me), update_sem.at[0])
    drain(update_ref.at[:, 0 : chips * bs], passed_sem)
    for copy in results:
        copy.wait()

    @pl.when(ids_self)
    def _():
        drain(masked.at[0 : depth - 1], send_sem.at[0])

    @pl.when(jnp.logical_not(ids_self))
    def _():
        drain(masked, send_sem.at[0])

    for h in range(HALVES):
        drain(raw.at[h, 0 : plane - 1], send_sem.at[1])
    drain(xr.at[0, 0 : chips - 1], send_sem.at[2])
    drain(xr.at[0], send_sem.at[11])
    drain(yr.at[0, 0 : chips - 1], send_sem.at[3])
    drain(yr.at[0], send_sem.at[3])
    drain(up.at[:, 0:half], send_sem.at[4])
    if half > 1:
        drain(down.at[:, 0 : half - 1], send_sem.at[5])
    drain(parts.at[0 : depth - 1], send_sem.at[6])
    drain(grad.at[0 : depth - 1], send_sem.at[7])
    drain(update_ref.at[:, 0 : (plane - 1) * bs], send_sem.at[8])
    drain(stats.at[0 : GROUP - 1], send_sem.at[9])

    @pl.when(jnp.logical_not(piece_self))
    def _():
        drain(final, send_sem.at[10])


def place_kernel(cuts, *refs):
    count = len(cuts)
    sources, places, held, sem = refs[:count], refs[count : 2 * count], refs[2 * count : 3 * count], refs[-1]
    moves = []
    for source, place, here, cut in zip(sources, places, held, cuts):
        rows = source.shape[0] // cut
        for k in range(cut):
            at = pl.ds(k * rows, rows)
            n = len(moves)
            moves.append(
                (
                    pltpu.make_async_copy(source.at[at], here.at[at], sem.at[0, n]),
                    pltpu.make_async_copy(here.at[at], place.at[at], sem.at[1, n]),
                )
            )
    for first, _ in moves:
        first.start()
    for first, second in moves:
        first.wait()
        second.start()
    for _, second in moves:
        second.wait()


def per_device(
    pooled_grad,
    bag_ids,
    bag_lengths,
    slot_table,
    layer_input,
    layer_grad_out,
    left_stats,
    right_stats,
    left_root,
    right_root,
    second_moment,
):
    depth = lax.axis_size("dp") // GROUP
    columns = lax.axis_size("blk")
    plane = columns * GROUP
    chips = plane // CORES
    shares = depth // columns
    half = depth // 2
    samples, tables, edim = pooled_grad.shape
    width = edim // HALVES
    bs = left_root.shape[2]
    share = left_stats.shape[2]
    kdim = layer_input.shape[1]
    ids = jnp.transpose(bag_ids, (0, 1, 2, 4, 3)).reshape(tables, POOL, samples)
    lengths = bag_lengths.reshape(tables, samples)
    smem = pl.BlockSpec(memory_space=pltpu.SMEM)
    hbm = pl.BlockSpec(memory_space=pl.ANY)
    dma = pltpu.SemaphoreType.DMA
    vmem = pltpu.VMEM
    shapes = (
        jax.ShapeDtypeStruct((bs, edim), F32),
        jax.ShapeDtypeStruct(left_stats.shape, F32),
        jax.ShapeDtypeStruct(right_stats.shape, F32),
        jax.ShapeDtypeStruct((1, share, GROUP * bs), F32),
        jax.ShapeDtypeStruct((bs, plane * bs), BF16),
    )
    cuts = (1, 1, 1, 1, 4)
    results = pl.pallas_call(
        functools.partial(exchange_kernel, depth, columns),
        out_shape=shapes,
        in_specs=[smem] + [hbm] * 10,
        out_specs=(hbm,) * 5,
        scratch_shapes=[
            vmem((samples, tables, edim), BF16),
            vmem((HALVES, samples * tables, width), F32),
            vmem((HALVES, plane, shares, samples, width), BF16),
            vmem((tables, POOL, samples), jnp.int32),
            vmem((tables, samples), jnp.int32),
            vmem((depth, XLO * POOL, CORES * samples), jnp.int32),
            vmem((shares, columns, XLO * POOL, CORES * samples), jnp.int32),
            vmem((shares, columns * bs, plane * samples), BF16),
            vmem((HALVES, plane, shares, samples, width), BF16),
            vmem((HALVES, depth, bs, width), F32),
            vmem((HALVES, half + 1, bs, width), F32),
            vmem((HALVES, half, bs, width), F32),
            vmem((HALVES, bs, width), F32),
            vmem((CORES, chips, samples, kdim), BF16),
            vmem((CORES, chips, samples, bs), BF16),
            vmem((depth, bs // depth, bs), F32),
            vmem((depth, bs // depth, bs), F32),
            vmem((bs // depth, bs), F32),
            vmem((depth, bs // depth, bs), F32),
            vmem((bs, bs), F32),
            vmem((bs, bs), F32),
            vmem((bs, bs), F32),
            vmem((GROUP, 3, 8, bs), F32),
            vmem((GROUP, 3, 8, bs), F32),
            vmem((bs, bs), BF16),
            vmem((bs, bs), F32),
            vmem((bs, bs), F32),
            vmem((bs, bs), F32),
            vmem(left_stats.shape, F32),
            vmem(right_stats.shape, F32),
            vmem(left_stats.shape, F32),
            vmem(right_stats.shape, F32),
            vmem((1, share, GROUP * bs), F32),
            dma((8,)),
            dma((7,)),
            dma((3,)),
            dma,
            dma((HALVES,)),
            dma((2,)),
            dma,
            dma((HALVES, half + 1, SUBS)),
            dma((HALVES, half, SUBS)),
            dma,
            dma,
            dma,
            dma,
            dma((chips,)),
            dma,
            dma((12,)),
        ],
        compiler_params=pltpu.CompilerParams(
            collective_id=0, has_side_effects=True, vmem_limit_bytes=56 * 1024 * 1024
        ),
        name="exchange",
    )(
        slot_table,
        pooled_grad,
        ids,
        lengths,
        layer_input,
        layer_grad_out,
        left_stats,
        right_stats,
        left_root,
        right_root,
        second_moment,
    )
    table, left_new, right_new, moment_new, update = pl.pallas_call(
        functools.partial(place_kernel, cuts),
        out_shape=shapes,
        in_specs=[hbm] * 5,
        out_specs=(hbm,) * 5,
        scratch_shapes=[vmem(one.shape, one.dtype) for one in shapes] + [dma((2, sum(cuts)))],
        compiler_params=pltpu.CompilerParams(vmem_limit_bytes=56 * 1024 * 1024),
        name="place",
    )(*results)
    return table[None], left_new, right_new, moment_new, update[None]


def solution(mesh):
    placed = (
        P(("dp", "blk"), None, None),
        P("dp", None, "blk", None, None),
        P("dp", None, "blk", None),
        P(),
        P(("dp", "blk"), None),
        P(("dp", "blk"), None),
        P("blk", None, "dp", None),
        P("blk", None, "dp", None),
        P("blk", None, None, None),
        P("blk", None, None, None),
        P(None, None, "blk"),
    )
    return jax.shard_map(
        per_device,
        mesh=mesh,
        in_specs=placed,
        out_specs=(
            P("dp", "blk", None),
            P("blk", None, "dp", None),
            P("blk", None, "dp", None),
            P(None, "dp", "blk"),
            P(),
        ),
        check_vma=False,
    )
```

```python
import functools

import jax
import jax.numpy as jnp
from jax import lax
from jax.experimental import pallas as pl
from jax.experimental.pallas import tpu as pltpu
from jax.sharding import PartitionSpec as P

MESH = pl.DeviceIdType.MESH
F32, BF16 = jnp.float32, jnp.bfloat16
CORES, XLO = 2, 2
GROUP = CORES * XLO
POOL = 4
HALVES = 2
LAG = 2
SUBS = 2
DENSE_MID = False

second_beta = 0.9
graft_epsilon = 1e-08
tiny = 1e-30
steps_16 = 32000.0
norm_epsilon = 1e-06
highest = lax.Precision.HIGHEST


def exchange_kernel(
    depth,
    columns,
    slots_ref,
    pooled_ref,
    ids_ref,
    lengths_ref,
    x_ref,
    y_ref,
    left_stats_ref,
    right_stats_ref,
    left_root_ref,
    right_root_ref,
    moment_ref,
    table_ref,
    left_ref,
    right_ref,
    moment_new_ref,
    update_ref,
    pooled,
    wide,
    ordered,
    ids_in,
    lengths_in,
    masked,
    idr,
    onehot,
    raw,
    own,
    given,
    up,
    down,
    final,
    coded,
    steps_out,
    coded_in,
    steps_in,
    table_out,
    xr,
    yr,
    part,
    parts,
    own_sum,
    grad,
    lmat,
    rmat,
    mmat,
    stage,
    stats,
    block_update,
    left_root,
    right_root,
    moment_in,
    left_stats,
    right_stats,
    left_out,
    right_out,
    moment_out,
    pooled_sem,
    in_sem,
    out_sem,
    ids_sem,
    raw_sem,
    x_sem,
    y_sem,
    given_sem,
    up_sem,
    down_sem,
    coded_sem,
    steps_sem,
    table_sem,
    parts_sem,
    grad_sem,
    stats_sem,
    update_sem,
    passed_sem,
    send_sem,
):
    plane = columns * GROUP
    chips = plane // CORES
    shares = depth // columns
    half = depth // 2
    bs = lmat.shape[1]
    share = left_ref.shape[2]
    samples, tables, edim = pooled.shape
    width = edim // HALVES
    kdim = plane * samples
    dp, blk = lax.axis_index("dp"), lax.axis_index("blk")
    core = dp % CORES
    z = (dp // CORES) % depth
    xl = dp // (CORES * depth)
    g = xl * CORES + core
    me = blk * GROUP + g
    chip = me // CORES
    wide_bs = CORES * bs

    def dp_of(xl_of, z_of, core_of):
        return (xl_of * depth + z_of) * CORES + core_of

    def in_plane(q):
        other = q % GROUP
        return (dp_of(other // CORES, z, other % CORES), q // GROUP)

    def along_z(z_of):
        return (dp_of(xl, z_of, core), blk)

    def same_core(chip_of):
        return in_plane(chip_of * CORES + core)

    twin = in_plane(chip * CORES + 1 - core)

    def loop(first, last, body):
        def step(k, carry):
            body(k)
            return carry

        lax.fori_loop(first, last, step, 0)

    def remote(src, dst, sent, arrived, device):
        return pltpu.make_async_remote_copy(
            src_ref=src, dst_ref=dst, send_sem=sent, recv_sem=arrived, device_id=device, device_id_type=MESH
        )

    def drain(ref, sem):
        pltpu.make_async_copy(ref, ref, sem).wait()

    chunks = pooled_sem.shape[0]
    per_chunk = samples // chunks

    def pooled_copy(k):
        rows = pl.ds(k * per_chunk, per_chunk)
        return pltpu.make_async_copy(pooled_ref.at[rows], pooled.at[rows], pooled_sem.at[k])

    local = [
        pltpu.make_async_copy(src, dst, in_sem.at[k])
        for k, (src, dst) in enumerate(
            (
                (ids_ref, ids_in),
                (lengths_ref, lengths_in),
                (left_root_ref.at[pl.ds(xl * CORES, CORES), 0], left_root),
                (right_root_ref.at[pl.ds(xl * CORES, CORES), 0], right_root),
                (moment_ref.at[0, :, pl.ds(pl.multiple_of(xl * wide_bs, wide_bs), wide_bs)], moment_in),
                (left_stats_ref, left_stats),
                (right_stats_ref, right_stats),
            )
        )
    ]
    loop(0, chunks, lambda k: pooled_copy(k).start())
    for copy in local:
        copy.start()

    ids_self = blk == z // shares
    piece_z = blk * shares + z // columns
    piece_blk = z % columns
    piece_self = jnp.logical_and(piece_z == z, piece_blk == blk)
    from_z = (z % shares) * columns + blk
    from_blk = z // shares

    barrier = pltpu.get_barrier_semaphore()

    def greet(device):
        pl.semaphore_signal(barrier, inc=1, device_id=device, device_id_type=MESH)

    loop(1, plane, lambda o: greet(in_plane((me + o) % plane)))
    loop(1, depth, lambda o: greet(along_z((z + o) % depth)))

    def greet_ids(k):
        z_of, blk_of = blk * shares + k // columns, k % columns

        @pl.when(jnp.logical_not(jnp.logical_and(z_of == z, blk_of == blk)))
        def _():
            greet((dp_of(xl, z_of, core), blk_of))

    loop(0, depth, greet_ids)

    @pl.when(jnp.logical_not(piece_self))
    def _():
        greet((dp_of(xl, from_z, 1), from_blk))

    local[0].wait()
    local[1].wait()
    position = lax.broadcasted_iota(jnp.int32, (POOL, samples), 0)

    def mask(z_of):
        for x_of in range(XLO):
            for core_of in range(CORES):
                source = dp_of(x_of, z_of, core_of)
                bag = lengths_in[pl.ds(source, 1), :]
                kept = jnp.where(position < bag, ids_in[source], -1)
                masked[z_of, x_of * POOL : (x_of + 1) * POOL, core_of * samples : (core_of + 1) * samples] = kept

    loop(0, depth, mask)

    def widen(h):
        def one(s):
            rows = pl.ds(pl.multiple_of(s * tables, tables), tables)
            wide[h, rows, :] = pooled[s, :, h * width : (h + 1) * width].astype(F32)

        return one

    def widen_first(k):
        pooled_copy(k).wait()
        loop(k * per_chunk, (k + 1) * per_chunk, widen(0))

    loop(0, chunks, widen_first)

    greetings = (plane - 1) + (depth - 1) + depth - ids_self.astype(jnp.int32)
    pl.semaphore_wait(barrier, greetings + CORES * core * jnp.logical_not(piece_self).astype(jnp.int32))

    def send_ids(k):
        z_of = (z + k) % depth
        itself = jnp.logical_and(z_of == z, ids_self)
        place = idr.at[z % shares, blk]

        @pl.when(itself)
        def _():
            pltpu.make_async_copy(masked.at[z_of], place, ids_sem).start()

        @pl.when(jnp.logical_not(itself))
        def _():
            remote(masked.at[z_of], place, send_sem.at[0], ids_sem, (dp_of(xl, z_of, core), z // shares)).start()

    loop(0, depth, send_ids)

    def rows_of(h, q, i):
        other = q % GROUP
        slot = dp_of(other // CORES, (q // GROUP) * shares + i, other % CORES)
        return wide[h, pl.ds(slots_ref[slot], samples, stride=tables), :].astype(BF16)

    def send_raw(h):
        def one(o):
            q = (me + o) % plane
            for i in range(shares):
                ordered[h, q, i] = rows_of(h, q, i)
            remote(ordered.at[h, q], raw.at[h, me], send_sem.at[1], raw_sem.at[h], in_plane(q)).start()

        loop(1, plane, one)
        for i in range(shares):
            raw[h, me, i] = rows_of(h, me, i)

    def y_part(chip_of):
        return y_ref.at[:, pl.ds(pl.multiple_of(chip_of * wide_bs, wide_bs), wide_bs)]

    def send_dense():
        @pl.when(core == 0)
        def _():
            pltpu.make_async_copy(x_ref, xr.at[me], x_sem).start()
            pltpu.make_async_copy(y_part(chip), yr.at[me], y_sem).start()

        @pl.when(core == 1)
        def _():
            remote(x_ref, xr.at[me], send_sem.at[2], x_sem, twin).start()
            remote(y_part(chip), yr.at[me], send_sem.at[3], y_sem, twin).start()

        def one(o):
            to = (chip + o) % chips
            remote(x_ref, xr.at[me], send_sem.at[2], x_sem, in_plane(to * CORES)).start()
            remote(y_part(to), yr.at[me], send_sem.at[3], y_sem, in_plane(to * CORES)).start()

        loop(1, chips, one)

    send_raw(0)
    if DENSE_MID:
        send_dense()
    loop(0, samples, widen(1))
    send_raw(1)
    if not DENSE_MID:
        send_dense()

    drain(idr, ids_sem)
    rows = lax.broadcasted_iota(jnp.int32, (bs, 128), 0)

    def weigh(k):
        i, source = k // columns, k % columns
        tile = idr[i, source]
        for x_of in range(XLO):
            ids = [tile[x_of * POOL + p : x_of * POOL + p + 1, :] for p in range(POOL)]
            length = sum((one >= 0).astype(jnp.int32) for one in ids)
            value = jnp.where(length == 1, 12.0, jnp.where(length == 2, 6.0, jnp.where(length == 3, 4.0, 3.0)))
            value = jnp.broadcast_to(value, (bs, 128))
            place = pl.ds(pl.multiple_of((source * XLO + x_of) * 128, 128), 128)
            ids = [jnp.broadcast_to(one, (bs, 128)) - rows for one in ids]
            for rb in range(columns):
                weight = jnp.zeros((bs, 128), F32)
                for one in ids:
                    weight = weight + jnp.where(one == rb * bs, value, 0.0)
                onehot[i, rb * bs : (rb + 1) * bs, place] = weight.astype(BF16)

    loop(0, shares * columns, weigh)

    def product(h, i):
        whole = jnp.dot(onehot[i], raw[h, :, i].reshape(kdim, width), preferred_element_type=F32)
        own[h, pl.ds(i * columns, columns)] = whole.reshape(columns, bs, width)

    def product_of(h, p):
        i, rb = p // columns, p % columns
        weights = onehot[i, pl.ds(pl.multiple_of(rb * bs, bs), bs), :]
        own[h, p] = jnp.dot(weights, raw[h, :, i].reshape(kdim, width), preferred_element_type=F32)

    sub = bs // SUBS

    def rows_at(s):
        return pl.ds(s * sub, sub)

    def send_up(h, lane, t, s):
        there = up.at[h, lane, t + 1, rows_at(s)]
        remote(
            up.at[h, lane, t, rows_at(s)],
            there,
            send_sem.at[4],
            up_sem.at[h, lane, t + 1, s],
            along_z((z + 1) % depth),
        ).start()

    def send_down(h, lane, t, s):
        there = down.at[h, lane, t + 1, rows_at(s)]
        remote(
            down.at[h, lane, t, rows_at(s)],
            there,
            send_sem.at[5],
            down_sem.at[h, lane, t + 1, s],
            along_z((z + depth - 1) % depth),
        ).start()

    def piece_up(t):
        return (z + half - t + depth) % depth

    def piece_down(t):
        return (z - (half - 1) + t + depth) % depth

    def wait_up(h, lane, t, s):
        drain(up.at[h, lane, t, rows_at(s)], up_sem.at[h, lane, t, s])

    def wait_down(h, lane, t, s):
        drain(down.at[h, lane, t, rows_at(s)], down_sem.at[h, lane, t, s])

    def hand_over(h, p):
        remote(own.at[h, p], given.at[h, p], send_sem.at[12], given_sem.at[h, p], twin).start()

    def feed_all(h):
        drain(raw.at[h, 0 : plane - 1], raw_sem.at[h])
        for k in range(shares):
            product(h, (piece_up(0) // columns + k) % shares)
            if k == 0:
                hand_over(h, piece_up(0))

        def one(t):
            @pl.when(t > 0)
            def _():
                hand_over(h, piece_up(t))

            hand_over(h, piece_down(t))

        loop(0, half, one)

    def feed(h):
        def one(t):
            product_of(h, piece_up(t))
            hand_over(h, piece_up(t))
            product_of(h, piece_down(t))
            hand_over(h, piece_down(t))

        return one

    def arrive(h, p):
        drain(given.at[h, p], given_sem.at[h, p])

    def begin(h):
        drain(raw.at[h, 0 : plane - 1], raw_sem.at[h])
        if h == 0:
            for k in range(shares):
                product(h, (piece_up(0) // columns + k) % shares)
        else:
            product_of(h, piece_up(0))
            product_of(h, piece_down(0))
        for lane in (1, 0):
            source = given if lane == 0 else own
            if lane == 0:
                arrive(h, piece_up(0))
            up[h, lane, 0] = source[h, piece_up(0)]
            for s in range(SUBS):
                send_up(h, lane, 0, s)
            if lane == 0:
                arrive(h, piece_down(0))
            down[h, lane, 0] = source[h, piece_down(0)]
            if half > 1:
                for s in range(SUBS):
                    send_down(h, lane, 0, s)

    def hop(h, t):
        if h > 0:
            product_of(h, piece_up(t))
            product_of(h, piece_down(t))
        arrive(h, piece_up(t))
        arrive(h, piece_down(t))
        for s in range(SUBS):
            for lane in (1, 0):
                source = given if lane == 0 else own
                wait_up(h, lane, t, s)
                up[h, lane, t, rows_at(s)] += source[h, piece_up(t), rows_at(s)]
                send_up(h, lane, t, s)
                wait_down(h, lane, t, s)
                down[h, lane, t, rows_at(s)] += source[h, piece_down(t), rows_at(s)]
                send_down(h, lane, t, s)

    def last(h):
        t = half - 1
        if h > 0:
            product_of(h, piece_up(t))
            product_of(h, z)
        if half > 1:
            arrive(h, piece_up(t))
            arrive(h, z)
        for s in range(SUBS):
            for lane in (1, 0):
                source = given if lane == 0 else own
                wait_up(h, lane, t, s)
                up[h, lane, t, rows_at(s)] += source[h, piece_up(t), rows_at(s)]
                send_up(h, lane, t, s)
        for s in range(SUBS):
            for lane in (1, 0):
                source = given if lane == 0 else own
                wait_down(h, lane, t, s)
                final[h, lane, rows_at(s)] = down[h, lane, t, rows_at(s)] + source[h, z, rows_at(s)]

    def finish(h):
        for lane in (1, 0):
            for s in range(SUBS):
                wait_up(h, lane, half, s)
            total = (final[h, lane] + up[h, lane, half]) * (1.0 / 12.0)
            step = jnp.maximum(jnp.max(jnp.abs(total), axis=0, keepdims=True), tiny) * (1.0 / steps_16)
            scaled = total / step
            whole = (scaled + jnp.where(scaled >= 0.0, 0.5, -0.5)).astype(jnp.int32)
            coded[h, lane] = whole.astype(jnp.int16)
            steps_out[h, lane] = jnp.broadcast_to(step, (8, width))
            moves = (
                (coded.at[h, lane], coded_in.at[h], coded_sem.at[h]),
                (steps_out.at[h, lane], steps_in.at[h], steps_sem.at[h]),
            )

            def away(device, moves=moves):
                for k, (src, dst, sem) in enumerate(moves):
                    remote(src, dst, send_sem.at[10 + k], sem, device).start()

            @pl.when(piece_self)
            def _(moves=moves, away=away, lane=lane):
                if lane == 1:
                    for src, dst, sem in moves:
                        pltpu.make_async_copy(src, dst, sem).start()
                else:
                    away(twin)

            @pl.when(jnp.logical_not(piece_self))
            def _(away=away, lane=lane):
                away((dp_of(xl, piece_z, lane), piece_blk))

    def store_table():
        for h in range(HALVES):
            drain(coded_in.at[h], coded_sem.at[h])
            drain(steps_in.at[h], steps_sem.at[h])
            values = coded_in[h].astype(jnp.int32).astype(F32)
            table_out[:, h * width : (h + 1) * width] = values * steps_in[h, 0:1, :]
        pltpu.make_async_copy(table_out, table_ref, table_sem).start()

    def dense_one():
        drain(xr, x_sem)
        drain(yr, y_sem)
        partial = lax.dot_general(
            xr[...].reshape(kdim, bs),
            yr[...].reshape(kdim, wide_bs),
            (((0,), (0,)), ((), ())),
            preferred_element_type=F32,
        )
        part[...] = partial.reshape(part.shape)

        def one(o):
            z_of = (z + o) % depth
            remote(part.at[z_of], parts.at[z], send_sem.at[6], parts_sem, along_z(z_of)).start()

        loop(1, depth, one)

    def dense_two():
        drain(parts.at[0 : depth - 1], parts_sem)
        parts[z] = part[z]
        own_sum[...] = jnp.sum(parts[...], axis=0)

        def one(o):
            remote(own_sum, grad.at[z], send_sem.at[7], grad_sem, along_z((z + o) % depth)).start()

        loop(1, depth, one)

    def chip_place(chip_of):
        return update_ref.at[:, pl.ds(pl.multiple_of(chip_of * wide_bs, wide_bs), wide_bs)]

    def block_of(b):
        return grad[...].reshape(bs, wide_bs)[:, b * bs : (b + 1) * bs]

    def dense_three():
        drain(grad.at[0 : depth - 1], grad_sem)
        grad[z] = own_sum[...]
        for copy in local[2:5]:
            copy.wait()
        for b in range(CORES):
            cut = slice(b * bs, (b + 1) * bs)
            block = block_of(b)
            moment = second_beta * moment_in[:, cut] + (1.0 - second_beta) * block * block
            graft = block / (jnp.sqrt(moment) + graft_epsilon)
            halfway = jnp.dot(left_root[b], block, precision=highest, preferred_element_type=F32)
            precond = jnp.dot(halfway, right_root[b], precision=highest, preferred_element_type=F32)
            ratio = jnp.sqrt(jnp.sum(graft * graft) / (jnp.sum(precond * precond) + norm_epsilon))
            block_update[:, cut] = (precond * ratio).astype(BF16)
            mmat[b] = moment
        place = chip_place(chip)

        def one(o):
            to = in_plane(((chip + o) % chips) * CORES)
            remote(block_update, place, send_sem.at[8], update_sem.at[o], to).start()

        loop(1, chips, one)
        remote(block_update, place, send_sem.at[8], passed_sem, twin).start()
        pltpu.make_async_copy(block_update, place, update_sem.at[0]).start()

    def statistics():
        for b in range(CORES):
            block = block_of(b)
            lmat[b] = lax.dot_general(
                block, block, (((1,), (1,)), ((), ())), precision=highest, preferred_element_type=F32
            )
            rmat[b] = lax.dot_general(
                block, block, (((0,), (0,)), ((), ())), precision=highest, preferred_element_type=F32
            )
        stage[...] = jnp.zeros(stage.shape, F32)

        def rows_for(other):
            first = dp_of(other // CORES, z, other % CORES) * share
            for b in range(CORES):
                for kind, matrix in enumerate((lmat, rmat, mmat)):
                    for r in range(share):
                        stage[other, b, kind, r : r + 1, :] = matrix[b, pl.ds(first + r, 1), :]

        loop(0, GROUP, rows_for)
        place = stats.at[pl.ds(xl * CORES, CORES)]
        pltpu.make_async_copy(stage.at[g], place, stats_sem).start()

        def one_group(o):
            other = (g + o) % GROUP
            remote(stage.at[other], place, send_sem.at[9], stats_sem, in_plane(blk * GROUP + other)).start()

        loop(1, GROUP, one_group)

    def pass_update():
        def one(o):
            place = chip_place((chip + chips - o) % chips)
            pltpu.make_async_copy(place, place, update_sem.at[o]).wait()
            remote(place, place, send_sem.at[8], passed_sem, twin).start()

        loop(1, chips, one)

    results = (
        pltpu.make_async_copy(left_out, left_ref, out_sem.at[0]),
        pltpu.make_async_copy(right_out, right_ref, out_sem.at[1]),
        pltpu.make_async_copy(moment_out, moment_new_ref, out_sem.at[2]),
    )

    def store_statistics():
        local[5].wait()
        local[6].wait()
        drain(stats, stats_sem)
        for other in range(GROUP):
            left_out[other, 0] = left_stats[other, 0] + stats[other, 0, 0:share, :]
            right_out[other, 0] = right_stats[other, 0] + stats[other, 1, 0:share, :]
            moment_out[0, :, other * bs : (other + 1) * bs] = stats[other, 2, 0:share, :]
        for copy in results:
            copy.start()

    lag = min(LAG, half + 1)
    end = half + lag

    def kind(t):
        return "" if t < 0 or t > half else "b" if t == 0 else "f" if t == half else "l" if t == half - 1 else "h"

    def ring():
        step = 0
        while step <= end:
            kinds = (kind(step), kind(step - lag))
            stop = step + 1
            while stop <= end and "h" in kinds and (kind(stop), kind(stop - lag)) == kinds:
                stop += 1

            def run(t, kinds=kinds):
                for h, what in enumerate(kinds):
                    if what == "b":
                        begin(h)
                    elif what == "h":
                        hop(h, t - h * lag)
                    elif what == "l":
                        last(h)
                    elif what == "f":
                        finish(h)

            if stop - step > 1:
                loop(step, stop, run)
            else:
                run(step)
            step = stop

    def dense():
        feed_all(0)
        if DENSE_MID:
            dense_one()
            dense_two()
        drain(raw.at[1, 0 : plane - 1], raw_sem.at[1])
        loop(0, half, feed(1))
        if not DENSE_MID:
            dense_one()
            dense_two()
        dense_three()
        statistics()
        pass_update()

    @pl.when(core == 0)
    def _():
        dense()
        drain(xr.at[0 : chips - 1], send_sem.at[2])
        drain(yr.at[0 : chips - 1], send_sem.at[3])
        drain(own, send_sem.at[12])
        drain(parts.at[0 : depth - 1], send_sem.at[6])
        drain(grad.at[0 : depth - 1], send_sem.at[7])
        drain(chip_place(chip), update_sem.at[0])
        for _ in range(CORES):
            drain(update_ref.at[:, 0 : (chips - 1) * wide_bs], send_sem.at[8])
        drain(chip_place(0), send_sem.at[8])
        drain(stage.at[0 : GROUP - 1], send_sem.at[9])

    @pl.when(core == 1)
    def _():
        ring()
        for copy in local[2:5]:
            copy.wait()
        drain(update_ref, passed_sem)
        drain(xr.at[0:chips], send_sem.at[2])
        drain(yr.at[0:chips], send_sem.at[3])
        drain(up.at[:, :, 0:half], send_sem.at[4])
        if half > 1:
            drain(down.at[:, :, 0 : half - 1], send_sem.at[5])

        @pl.when(jnp.logical_not(piece_self))
        def _():
            drain(coded, send_sem.at[10])
            drain(steps_out, send_sem.at[11])

        @pl.when(piece_self)
        def _():
            drain(coded.at[:, 0], send_sem.at[10])
            drain(steps_out.at[:, 0], send_sem.at[11])

    store_statistics()
    store_table()
    drain(table_ref, table_sem)
    for copy in results:
        copy.wait()

    @pl.when(ids_self)
    def _():
        drain(masked.at[0 : depth - 1], send_sem.at[0])

    @pl.when(jnp.logical_not(ids_self))
    def _():
        drain(masked, send_sem.at[0])

    for h in range(HALVES):
        drain(raw.at[h, 0 : plane - 1], send_sem.at[1])


def place_kernel(cuts, *refs):
    count = len(cuts)
    sources, places, held, sem = refs[:count], refs[count : 2 * count], refs[2 * count : 3 * count], refs[-1]
    moves = []
    for source, place, here, cut in zip(sources, places, held, cuts):
        rows = source.shape[0] // cut
        for k in range(cut):
            at = pl.ds(k * rows, rows)
            n = len(moves)
            moves.append(
                (
                    pltpu.make_async_copy(source.at[at], here.at[at], sem.at[0, n]),
                    pltpu.make_async_copy(here.at[at], place.at[at], sem.at[1, n]),
                )
            )
    for first, _ in moves:
        first.start()
    for first, second in moves:
        first.wait()
        second.start()
    for _, second in moves:
        second.wait()


def per_device(
    pooled_grad,
    bag_ids,
    bag_lengths,
    slot_table,
    layer_input,
    layer_grad_out,
    left_stats,
    right_stats,
    left_root,
    right_root,
    second_moment,
):
    depth = lax.axis_size("dp") // GROUP
    columns = lax.axis_size("blk")
    plane = columns * GROUP
    chips = plane // CORES
    shares = depth // columns
    half = depth // 2
    samples, tables, edim = pooled_grad.shape
    width = edim // HALVES
    bs = left_root.shape[2]
    share = left_stats.shape[2]
    kdim = layer_input.shape[1]
    ids = jnp.transpose(bag_ids, (0, 1, 2, 4, 3)).reshape(tables, POOL, samples)
    lengths = bag_lengths.reshape(tables, samples)
    smem = pl.BlockSpec(memory_space=pltpu.SMEM)
    hbm = pl.BlockSpec(memory_space=pl.ANY)
    dma = pltpu.SemaphoreType.DMA
    vmem = pltpu.VMEM
    shapes = (
        jax.ShapeDtypeStruct((bs, edim), F32),
        jax.ShapeDtypeStruct(left_stats.shape, F32),
        jax.ShapeDtypeStruct(right_stats.shape, F32),
        jax.ShapeDtypeStruct((1, share, GROUP * bs), F32),
        jax.ShapeDtypeStruct((bs, plane * bs), BF16),
    )
    cuts = (1, 1, 1, 1, 4)
    results = pl.pallas_call(
        functools.partial(exchange_kernel, depth, columns),
        out_shape=shapes,
        in_specs=[smem] + [hbm] * 10,
        out_specs=(hbm,) * 5,
        scratch_shapes=[
            vmem((samples, tables, edim), BF16),
            vmem((HALVES, samples * tables, width), F32),
            vmem((HALVES, plane, shares, samples, width), BF16),
            vmem((tables, POOL, samples), jnp.int32),
            vmem((tables, samples), jnp.int32),
            vmem((depth, XLO * POOL, CORES * samples), jnp.int32),
            vmem((shares, columns, XLO * POOL, CORES * samples), jnp.int32),
            vmem((shares, columns * bs, plane * samples), BF16),
            vmem((HALVES, plane, shares, samples, width), BF16),
            vmem((HALVES, depth, bs, width), F32),
            vmem((HALVES, depth, bs, width), F32),
            vmem((HALVES, CORES, half + 1, bs, width), F32),
            vmem((HALVES, CORES, half, bs, width), F32),
            vmem((HALVES, CORES, bs, width), F32),
            vmem((HALVES, CORES, bs, width), jnp.int16),
            vmem((HALVES, CORES, 8, width), F32),
            vmem((HALVES, bs, width), jnp.int16),
            vmem((HALVES, 8, width), F32),
            vmem((bs, edim), F32),
            vmem((plane, samples, kdim), BF16),
            vmem((plane, samples, CORES * bs), BF16),
            vmem((depth, bs // depth, CORES * bs), F32),
            vmem((depth, bs // depth, CORES * bs), F32),
            vmem((bs // depth, CORES * bs), F32),
            vmem((depth, bs // depth, CORES * bs), F32),
            vmem((CORES, bs, bs), F32),
            vmem((CORES, bs, bs), F32),
            vmem((CORES, bs, bs), F32),
            vmem((GROUP, CORES, 3, 8, bs), F32),
            vmem((GROUP, 3, 8, bs), F32),
            vmem((bs, CORES * bs), BF16),
            vmem((CORES, bs, bs), F32),
            vmem((CORES, bs, bs), F32),
            vmem((bs, CORES * bs), F32),
            vmem(left_stats.shape, F32),
            vmem(right_stats.shape, F32),
            vmem(left_stats.shape, F32),
            vmem(right_stats.shape, F32),
            vmem((1, share, GROUP * bs), F32),
            dma((8,)),
            dma((7,)),
            dma((3,)),
            dma,
            dma((HALVES,)),
            dma,
            dma,
            dma((HALVES, depth)),
            dma((HALVES, CORES, half + 1, SUBS)),
            dma((HALVES, CORES, half, SUBS)),
            dma((HALVES,)),
            dma((HALVES,)),
            dma,
            dma,
            dma,
            dma,
            dma((chips,)),
            dma,
            dma((13,)),
        ],
        compiler_params=pltpu.CompilerParams(
            collective_id=0, has_side_effects=True, vmem_limit_bytes=56 * 1024 * 1024
        ),
        name="exchange",
    )(
        slot_table,
        pooled_grad,
        ids,
        lengths,
        layer_input,
        layer_grad_out,
        left_stats,
        right_stats,
        left_root,
        right_root,
        second_moment,
    )
    table, left_new, right_new, moment_new, update = pl.pallas_call(
        functools.partial(place_kernel, cuts),
        out_shape=shapes,
        in_specs=[hbm] * 5,
        out_specs=(hbm,) * 5,
        scratch_shapes=[vmem(one.shape, one.dtype) for one in shapes] + [dma((2, sum(cuts)))],
        compiler_params=pltpu.CompilerParams(vmem_limit_bytes=56 * 1024 * 1024),
        name="place",
    )(*results)
    return table[None], left_new, right_new, moment_new, update[None]


def solution(mesh):
    placed = (
        P(("dp", "blk"), None, None),
        P("dp", None, "blk", None, None),
        P("dp", None, "blk", None),
        P(),
        P(("dp", "blk"), None),
        P(("dp", "blk"), None),
        P("blk", None, "dp", None),
        P("blk", None, "dp", None),
        P("blk", None, None, None),
        P("blk", None, None, None),
        P(None, None, "blk"),
    )
    return jax.shard_map(
        per_device,
        mesh=mesh,
        in_specs=placed,
        out_specs=(
            P("dp", "blk", None),
            P("blk", None, "dp", None),
            P("blk", None, "dp", None),
            P(None, "dp", "blk"),
            P(),
        ),
        check_vma=False,
    )
```
